32 devices in a mesh: space: 8 (over y, x, core), ens: 4 (over z).
Axes of the slice: x: 2, y: 2, z: 4, core: 2. Of those that a mesh axis runs over, the one named last changes fastest.
Arguments:
- fields: bfloat16 [8, 45, 64, 360], P('ens', None, 'space'), may hold values from -6 to 6
- observed: bfloat16 [45, 64, 360], P(None, 'space'), may hold values from -8 to 8
- kernel_one: bfloat16 [9, 45, 5, 45], replicated, may hold values from -0.375 to 0.375
- bias_one: float32 [45], replicated, may hold values from -3 to 3
- kernel_two: bfloat16 [9, 45, 5, 45], replicated, may hold values from -0.375 to 0.375
- bias_two: float32 [45], replicated, may hold values from -3 to 3
- band_offset: int32 [64], replicated, may hold values from -4 to 3, as said below
- band_width: int32 [64], replicated, may hold values from 2 to 9
Outputs:
- score_grad: bfloat16 [8, 45, 64, 360], P('ens', None, 'space')
The draws below stay inside these ranges and needn't reach their ends.
Inputs may be any that keep to these rules, and one draw needn't show every extreme that they name: band_offset[i] + band_width[i] - 1 <= 4 for every latitude.
All inputs are finite; a program needn't handle non-finite values.
Results may differ from the reference program's by a relative error of at most 0.0053.
Values may be sent and summed in bfloat16 or wider, within the bound.
A program may use at most 128 MiB of HBM per device.

```python
import jax
import jax.numpy as jnp
from jax import lax

C = 45
NLON = 360
RLAT = 4
QLON = 2
NLAT = 64
MEMBERS = 8


def band_pair(key):
    keyed = jax.random.fold_in(key, 7)
    key_a, key_b, key_c, key_d = jax.random.split(keyed, 4)
    widths = jax.random.randint(key_a, (NLAT,), 2, 2 * RLAT + 2)
    raw = jax.random.randint(key_b, (NLAT,), 0, 1 << 20)
    offsets = -RLAT + raw % (2 * RLAT + 2 - widths)
    first = jax.random.randint(key_c, (), 0, NLAT)
    second = (first + 1 + jax.random.randint(key_d, (), 0, NLAT - 1)) % NLAT
    index = jnp.arange(NLAT)
    widths = jnp.where(index == first, 2 * RLAT + 1, widths)
    offsets = jnp.where(index == first, -RLAT, offsets)
    widths = jnp.where(index == second, 2, widths)
    offsets = jnp.where(index == second, RLAT - 1, offsets)
    return (offsets.astype(jnp.int32), widths.astype(jnp.int32))


def draw_band_offset(key, part):
    return band_pair(key)[0]


def draw_band_width(key, part):
    return band_pair(key)[1]


def block_levels(stream_key, shape, shards, low, largest):
    def one(position, shards_of):
        heights = jax.random.uniform(jax.random.fold_in(jax.random.fold_in(stream_key, 6), position), (shards_of,), jnp.float32, low / len(shards), largest / len(shards))
        return jnp.repeat(jnp.exp(heights), shape[position] // shards_of).reshape((-1,) + (1,) * (len(shape) - position - 1))

    level = one(*shards[0])
    for cut in shards[1:]:
        level = level * one(*cut)
    return level


def scatter_about(key, dims, scale, bound, shards=(), kind=jnp.bfloat16):
    gain = block_levels(key, dims, shards, -0.22, 0.18) if shards else 1.0
    entries = jax.random.normal(key, dims, jnp.float32) * scale * gain
    return jnp.minimum(jnp.maximum(entries, -bound), bound).astype(kind)


def setup_inputs(seed: int = 0) -> dict:
    key_of = jax.random.split(jax.random.key(seed), 9)
    fields = scatter_about(key_of[0], (MEMBERS, C, NLAT, NLON), 1.0, 6.0, ((0, 4), (2, 8)))
    observed = scatter_about(key_of[1], (C, NLAT, NLON), 1.5, 8.0, ((1, 8),))
    kernel_one = scatter_about(key_of[2], (2 * RLAT + 1, C, 2 * QLON + 1, C), (C * (2 * QLON + 1)) ** -0.5, 0.375)
    bias_one = scatter_about(key_of[3], (C,), 0.5, 3.0, (), jnp.float32)
    kernel_two = scatter_about(key_of[4], (2 * RLAT + 1, C, 2 * QLON + 1, C), (C * (2 * QLON + 1)) ** -0.5, 0.375)
    bias_two = scatter_about(key_of[5], (C,), 0.5, 3.0, (), jnp.float32)
    band_offset = draw_band_offset(jax.random.fold_in(key_of[8], 71), 0)
    band_width = draw_band_width(jax.random.fold_in(key_of[8], 71), 0)
    return {"fields": fields, "observed": observed, "kernel_one": kernel_one, "bias_one": bias_one, "kernel_two": kernel_two, "bias_two": bias_two, "band_offset": band_offset, "band_width": band_width}


def band_table(band_offset, band_width, taps):
    reach = (taps - 1) // 2
    rel = lax.broadcasted_iota(jnp.int32, (taps, band_offset.shape[0]), 0) - reach
    inside = (rel >= band_offset[None, :]) & (rel < band_offset[None, :] + band_width[None, :])
    scale = lax.rsqrt(band_width.astype(jnp.float32))[None, :]
    return jnp.where(inside, scale, jnp.float32(0.0))

def convolve(padded, kernel, weights_rows):
    taps, chan, lon_taps = (kernel.shape[0], kernel.shape[1], kernel.shape[2])
    half = (lon_taps - 1) // 2
    rows = weights_rows.shape[1]
    total = jnp.zeros((chan, rows, padded.shape[2]), jnp.float32)
    for tap in range(taps):
        window = padded[:, tap:tap + rows, :]
        stacked = jnp.concatenate([jnp.roll(window, half - shift, axis=2) for shift in range(lon_taps)], axis=0)
        flat = kernel[tap].reshape(chan, lon_taps * chan).astype(jnp.float32)
        mixed = jnp.einsum('ok,klw->olw', flat, stacked.astype(jnp.float32))
        total = total + weights_rows[tap][None, :, None] * mixed
    return total

def phi(diff):
    return diff * lax.rsqrt(diff * diff + jnp.float32(0.25))

def reference(fields, observed, kernel_one, bias_one, kernel_two, bias_two, band_offset, band_width):
    taps = kernel_one.shape[0]
    reach = (taps - 1) // 2
    table = band_table(band_offset, band_width, taps)

    def member(field):
        padded = jnp.pad(field, ((0, 0), (reach, reach), (0, 0)))
        pre = convolve(padded, kernel_one, table)
        hidden = jax.nn.gelu(pre + bias_one[:, None, None]).astype(jnp.bfloat16)
        mixed = convolve(jnp.pad(hidden, ((0, 0), (reach, reach), (0, 0))), kernel_two, table)
        return (field.astype(jnp.float32) + mixed + bias_two[:, None, None]).astype(jnp.bfloat16)
    predicted = lax.map(member, fields)
    nlat = fields.shape[2]
    count = fields.shape[0]
    theta = jnp.pi * (jnp.arange(nlat, dtype=jnp.float32) + 0.5) / nlat - jnp.pi / 2
    weight = jnp.cos(theta)
    by_channel = jnp.swapaxes(predicted, 0, 1)

    def channel(pair):
        values, target = pair
        own = values.astype(jnp.float32)

        def step(index, acc):
            other = lax.dynamic_index_in_dim(own, index, 0, keepdims=False)
            return acc + phi(own - other[None])
        spread = lax.fori_loop(0, count, step, jnp.zeros_like(own))
        grad = phi(own - target.astype(jnp.float32)[None]) - spread / jnp.float32(count - 1)
        return (grad * weight[None, :, None]).astype(jnp.bfloat16)
    result = lax.map(channel, (by_channel, observed))
    return jnp.swapaxes(result, 0, 1)
```

```python
import functools

import jax
import jax.numpy as jnp
from jax import lax
from jax.experimental import pallas as pl
from jax.experimental.pallas import tpu as pltpu
from jax.sharding import PartitionSpec as P

MESH = pl.DeviceIdType.MESH
LANES = 128


def ceil_to(value, unit):
    return -(-value // unit) * unit


def phi(diff):
    return diff * lax.rsqrt(diff * diff + jnp.float32(0.25))


def kernel(
    dims,
    table,
    weight,
    x_ref,
    obs_ref,
    w1_ref,
    b1_ref,
    w2_ref,
    b2_ref,
    o_ref,
    taps_ref,
    acc,
    halo1,
    hid,
    halo2,
    pred,
    gath,
    grad,
    hs_sem,
    hr_sem,
    ps_sem,
    pr_sem,
    gs_sem,
    gr_sem,
):
    n_s, n_e, mem, rows, cp, lon, lp, taps, lt = dims
    reach = (taps - 1) // 2
    half = (lt - 1) // 2
    q = rows // n_e
    wide = mem * lp
    sp = lax.axis_index("space")
    en = lax.axis_index("ens")
    has_prev = sp > 0
    has_next = sp < n_s - 1

    def at_prev():
        return {"space": sp - 1, "ens": en}

    def at_next():
        return {"space": sp + 1, "ens": en}

    def peer(k):
        return lax.rem(en + k, n_e)

    barrier = pltpu.get_barrier_semaphore()

    @pl.when(has_prev)
    def _():
        pl.semaphore_signal(barrier, inc=1, device_id=at_prev(), device_id_type=MESH)

    @pl.when(has_next)
    def _():
        pl.semaphore_signal(barrier, inc=1, device_id=at_next(), device_id_type=MESH)

    for k in range(1, n_e):
        pl.semaphore_signal(
            barrier, inc=1, device_id={"space": sp, "ens": peer(k)}, device_id_type=MESH
        )
    count = n_e - 1 + jnp.where(has_prev, 1, 0) + jnp.where(has_next, 1, 0)
    pl.semaphore_wait(barrier, count)

    def halo_up(src, dst, stage):
        return pltpu.make_async_remote_copy(
            src_ref=src.at[pl.ds(0, reach)],
            dst_ref=dst.at[1],
            send_sem=hs_sem.at[stage, 0],
            recv_sem=hr_sem.at[stage, 0],
            device_id=at_prev(),
            device_id_type=MESH,
        )

    def halo_down(src, dst, stage):
        return pltpu.make_async_remote_copy(
            src_ref=src.at[pl.ds(rows - reach, reach)],
            dst_ref=dst.at[0],
            send_sem=hs_sem.at[stage, 1],
            recv_sem=hr_sem.at[stage, 1],
            device_id=at_next(),
            device_id_type=MESH,
        )

    def send_halo(src, dst, stage):
        @pl.when(has_prev)
        def _():
            halo_up(src, dst, stage).start()

        @pl.when(has_next)
        def _():
            halo_down(src, dst, stage).start()

    def recv_halo(src, dst, stage):
        @pl.when(has_prev)
        def _():
            halo_down(src, dst, stage).wait_recv()

        @pl.when(has_next)
        def _():
            halo_up(src, dst, stage).wait_recv()

        @pl.when(jnp.logical_not(has_prev))
        def _():
            dst[0] = jnp.zeros(dst.shape[1:], dst.dtype)

        @pl.when(jnp.logical_not(has_next))
        def _():
            dst[1] = jnp.zeros(dst.shape[1:], dst.dtype)

    def sent_halo(src, dst, stage):
        @pl.when(has_prev)
        def _():
            halo_up(src, dst, stage).wait_send()

        @pl.when(has_next)
        def _():
            halo_down(src, dst, stage).wait_send()

    def build(row, value):
        for mm in range(mem):
            part = value[:, mm * lp : (mm + 1) * lp]
            for s in range(lt):
                d = s - half
                moved = part if d == 0 else pltpu.roll(part, (-d) % lp, 1)
                taps_ref[row, pl.ds(s * cp, cp), pl.ds(mm * lp, lp)] = moved.astype(jnp.bfloat16)

    def conv_rows(w_ref, order):
        step = 256

        def body(n, carry):
            lane = pl.ds(pl.multiple_of(n * step, step), step)
            for r in order:
                lo, hi = max(0, r - rows + 1), min(taps - 1, r)
                y = jnp.dot(
                    w_ref[lo * cp : (hi + 1) * cp, :],
                    taps_ref[r, :, lane],
                    preferred_element_type=jnp.float32,
                )
                for t in range(lo, hi + 1):
                    i = r - t
                    acc[i, :, lane] += table[t, i] * y[(t - lo) * cp : (t - lo + 1) * cp]
            return carry

        lax.fori_loop(0, wide // step, body, 0)

    def conv(own, halo, w_ref, stage):
        acc[...] = jnp.zeros(acc.shape, jnp.float32)

        def own_row(r, carry):
            build(reach + r, own[r].astype(jnp.float32))
            return carry

        lax.fori_loop(0, rows, own_row, 0)
        conv_rows(w_ref, range(reach, reach + rows))
        recv_halo(own, halo, stage)

        def rim_row(r, carry):
            build(r, halo[0, r].astype(jnp.float32))
            build(reach + rows + r, halo[1, r].astype(jnp.float32))
            return carry

        lax.fori_loop(0, reach, rim_row, 0)
        conv_rows(w_ref, list(range(reach)) + list(range(reach + rows, 2 * reach + rows)))

    send_halo(x_ref, halo1, 0)
    conv(x_ref, halo1, w1_ref, 0)

    last = lp - LANES
    tail = lon - last

    def hidden_row(i, carry):
        for mm in range(mem):
            base = mm * lp
            h = jax.nn.gelu(acc[i, :, pl.ds(base, lp)] + b1_ref[...])
            first, end = h[:, :LANES], h[:, last:]
            spot = lax.broadcasted_iota(jnp.int32, end.shape, 1)
            after = pltpu.roll(first, tail, 1)
            before = pltpu.roll(end, LANES - tail, 1)
            wrap = jnp.where(spot < tail, end, jnp.where(spot < tail + half, after, before))
            hid[i, :, pl.ds(base, last)] = h[:, :last].astype(jnp.bfloat16)
            hid[i, :, pl.ds(base + last, LANES)] = wrap.astype(jnp.bfloat16)
        return carry

    lax.fori_loop(0, rows, hidden_row, 0)
    send_halo(hid, halo2, 1)
    conv(hid, halo2, w2_ref, 1)

    def pred_row(i, carry):
        for mm in range(mem):
            lane = pl.ds(mm * lp, lp)
            total = x_ref[i, :, lane].astype(jnp.float32) + acc[i, :, lane] + b2_ref[...]
            pred[i, :, lane] = total.astype(jnp.bfloat16)
        return carry

    lax.fori_loop(0, rows, pred_row, 0)

    def pred_copy(k, j, src_dev, dst_dev):
        return pltpu.make_async_remote_copy(
            src_ref=pred.at[dst_dev * q + j],
            dst_ref=gath.at[src_dev, j],
            send_sem=ps_sem.at[k, j],
            recv_sem=pr_sem.at[k, j],
            device_id={"space": sp, "ens": dst_dev},
            device_id_type=MESH,
        )

    def grad_copy(k, j, src_dev, dst_dev):
        return pltpu.make_async_remote_copy(
            src_ref=grad.at[dst_dev, j],
            dst_ref=o_ref.at[src_dev * q + j],
            send_sem=gs_sem.at[k, j],
            recv_sem=gr_sem.at[k, j],
            device_id={"space": sp, "ens": dst_dev},
            device_id_type=MESH,
        )

    for j in range(q):
        for k in range(1, n_e):
            pred_copy(k, j, en, peer(k)).start()
    for j in range(q):
        gath[en, j] = pred[en * q + j]
    members = n_e * mem
    for j in range(q):
        for k in range(1, n_e):
            pred_copy(k, j, peer(n_e - k), peer(k)).wait_recv()
        scale = weight[0, en * q + j]

        def part(step, carry):
            group, tile = step // (lp // LANES), step % (lp // LANES)
            chan = pl.ds(pl.multiple_of(group * 16, 16), 16)
            spots = [
                (a // mem, pl.ds(pl.multiple_of((a % mem) * lp + tile * LANES, LANES), LANES))
                for a in range(members)
            ]
            vals = [gath[dev, j, chan, lane].astype(jnp.float32) for dev, lane in spots]
            goal = obs_ref[
                j, chan, pl.ds(pl.multiple_of(tile * LANES, LANES), LANES)
            ].astype(jnp.float32)
            sums = [jnp.zeros((16, LANES), jnp.float32) for _ in range(members)]
            for a in range(members):
                for b in range(a + 1, members):
                    d = phi(vals[a] - vals[b])
                    sums[a] = sums[a] + d
                    sums[b] = sums[b] - d
            for a, (dev, lane) in enumerate(spots):
                g = phi(vals[a] - goal) - sums[a] * jnp.float32(1.0 / (members - 1))
                grad[dev, j, chan, lane] = (g * scale).astype(jnp.bfloat16)
            return carry

        lax.fori_loop(0, (cp // 16) * (lp // LANES), part, 0)
        for k in range(1, n_e):
            grad_copy(k, j, en, peer(k)).start()
        o_ref[en * q + j] = grad[en, j]
    sent_halo(x_ref, halo1, 0)
    sent_halo(hid, halo2, 1)
    for j in range(q):
        for k in range(1, n_e):
            pred_copy(k, j, en, peer(k)).wait_send()
            grad_copy(k, j, peer(n_e - k), peer(k)).wait_recv()
            grad_copy(k, j, en, peer(k)).wait_send()


def band_table(band_offset, band_width, taps):
    reach = (taps - 1) // 2
    rel = lax.broadcasted_iota(jnp.int32, (taps, band_offset.shape[0]), 0) - reach
    inside = (rel >= band_offset[None, :]) & (rel < band_offset[None, :] + band_width[None, :])
    scale = lax.rsqrt(band_width.astype(jnp.float32))[None, :]
    return jnp.where(inside, scale, jnp.float32(0.0))


def local(fields, observed, kernel_one, bias_one, kernel_two, bias_two, band_offset, band_width):
    mem, chan, rows, lon = fields.shape
    taps, _, lt, _ = kernel_one.shape
    reach, half = (taps - 1) // 2, (lt - 1) // 2
    n_s, n_e = lax.axis_size("space"), lax.axis_size("ens")
    q = rows // n_e
    cp, lp = ceil_to(chan, 16), ceil_to(lon + 2 * half, LANES)
    sp, en = lax.axis_index("space"), lax.axis_index("ens")
    base = sp * rows

    offset = lax.dynamic_slice_in_dim(band_offset, base, rows, 0)
    width = lax.dynamic_slice_in_dim(band_width, base, rows, 0)
    table = band_table(offset, width, taps)
    glob_rows = (base + lax.iota(jnp.int32, rows)).astype(jnp.float32)
    weight = jnp.cos(jnp.pi * (glob_rows + 0.5) / (rows * n_s) - jnp.pi / 2)[None]

    x = jnp.transpose(fields, (2, 1, 0, 3))
    gap = jnp.zeros((rows, chan, mem, lp - lon - 2 * half), x.dtype)
    x = jnp.concatenate([x, x[..., :half], gap, x[..., lon - half :]], axis=3)
    x = jnp.pad(x, ((0, 0), (0, cp - chan), (0, 0), (0, 0))).reshape(rows, cp, mem * lp)
    obs = lax.dynamic_slice_in_dim(observed, en * q, q, 1)
    obs = jnp.pad(jnp.transpose(obs, (1, 0, 2)), ((0, 0), (0, cp - chan), (0, lp - lon)))

    def flat(w):
        w = jnp.pad(w, ((0, 0), (0, cp - chan), (0, 0), (0, cp - chan)))
        return w.reshape(taps * cp, lt * cp)

    def column(b):
        return jnp.pad(b, (0, cp - chan))[:, None]

    dims = (n_s, n_e, mem, rows, cp, lon, lp, taps, lt)
    wide = mem * lp
    vmem = pl.BlockSpec(memory_space=pltpu.VMEM)
    smem = pl.BlockSpec(memory_space=pltpu.SMEM)
    bf16 = jnp.bfloat16
    out = pl.pallas_call(
        functools.partial(kernel, dims),
        out_shape=jax.ShapeDtypeStruct((rows, cp, wide), bf16),
        in_specs=[smem, smem] + [vmem] * 6,
        out_specs=vmem,
        scratch_shapes=[
            pltpu.VMEM((rows + 2 * reach, lt * cp, wide), bf16),
            pltpu.VMEM((rows, cp, wide), jnp.float32),
            pltpu.VMEM((2, reach, cp, wide), bf16),
            pltpu.VMEM((rows, cp, wide), bf16),
            pltpu.VMEM((2, reach, cp, wide), bf16),
            pltpu.VMEM((rows, cp, wide), bf16),
            pltpu.VMEM((n_e, q, cp, wide), bf16),
            pltpu.VMEM((n_e, q, cp, wide), bf16),
            pltpu.SemaphoreType.DMA((2, 2)),
            pltpu.SemaphoreType.DMA((2, 2)),
            pltpu.SemaphoreType.DMA((n_e, q)),
            pltpu.SemaphoreType.DMA((n_e, q)),
            pltpu.SemaphoreType.DMA((n_e, q)),
            pltpu.SemaphoreType.DMA((n_e, q)),
        ],
        compiler_params=pltpu.CompilerParams(
            collective_id=0, has_side_effects=True, vmem_limit_bytes=40 * 1024 * 1024
        ),
    )(
        table,
        weight,
        x,
        obs,
        flat(kernel_one),
        column(bias_one),
        flat(kernel_two),
        column(bias_two),
    )
    out = out.reshape(rows, cp, mem, lp)[:, :chan, :, :lon]
    return jnp.transpose(out, (2, 1, 0, 3))


def solution(mesh):
    in_specs = (P("ens", None, "space", None), P(None, "space", None), P(), P(), P(), P(), P(), P())
    out_specs = P("ens", None, "space", None)
    return jax.shard_map(local, mesh=mesh, in_specs=in_specs, out_specs=out_specs, check_vma=False)
```

```python
import functools

import jax
import jax.numpy as jnp
from jax import lax
from jax.experimental import pallas as pl
from jax.experimental.pallas import tpu as pltpu
from jax.sharding import PartitionSpec as P

MESH = pl.DeviceIdType.MESH
LANES = 128


def ceil_to(value, unit):
    return -(-value // unit) * unit


def phi(diff):
    return diff * lax.rsqrt(diff * diff + jnp.float32(0.25))


def kernel(
    dims,
    offset,
    width,
    weight,
    x_ref,
    obs_ref,
    w1_ref,
    b1_ref,
    w2_ref,
    b2_ref,
    o_ref,
    flat1,
    flat2,
    taps_ref,
    acc,
    halo1,
    hid,
    halo2,
    pred,
    gath,
    grad,
    hs_sem,
    hr_sem,
    ps_sem,
    pr_sem,
    gs_sem,
    gr_sem,
):
    n_s, n_e, mem, rows, cp, lon, lp, taps, lt = dims
    reach = (taps - 1) // 2
    half = (lt - 1) // 2
    q = rows // n_e
    sp = lax.axis_index("space")
    en = lax.axis_index("ens")
    has_prev = sp > 0
    has_next = sp < n_s - 1

    def at_prev():
        return {"space": sp - 1, "ens": en}

    def at_next():
        return {"space": sp + 1, "ens": en}

    def peer(k):
        return lax.rem(en + k, n_e)

    barrier = pltpu.get_barrier_semaphore()

    @pl.when(has_prev)
    def _():
        pl.semaphore_signal(barrier, inc=1, device_id=at_prev(), device_id_type=MESH)

    @pl.when(has_next)
    def _():
        pl.semaphore_signal(barrier, inc=1, device_id=at_next(), device_id_type=MESH)

    for k in range(1, n_e):
        pl.semaphore_signal(
            barrier, inc=1, device_id={"space": sp, "ens": peer(k)}, device_id_type=MESH
        )
    count = n_e - 1 + jnp.where(has_prev, 1, 0) + jnp.where(has_next, 1, 0)
    pl.semaphore_wait(barrier, count)

    def halo_up(src, dst, stage, mm):
        return pltpu.make_async_remote_copy(
            src_ref=src.at[mm, pl.ds(0, reach)],
            dst_ref=dst.at[mm, 1],
            send_sem=hs_sem.at[stage, 0, mm],
            recv_sem=hr_sem.at[stage, 0, mm],
            device_id=at_prev(),
            device_id_type=MESH,
        )

    def halo_down(src, dst, stage, mm):
        return pltpu.make_async_remote_copy(
            src_ref=src.at[mm, pl.ds(rows - reach, reach)],
            dst_ref=dst.at[mm, 0],
            send_sem=hs_sem.at[stage, 1, mm],
            recv_sem=hr_sem.at[stage, 1, mm],
            device_id=at_next(),
            device_id_type=MESH,
        )

    def send_halo(src, dst, stage, mm):
        @pl.when(has_prev)
        def _():
            halo_up(src, dst, stage, mm).start()

        @pl.when(has_next)
        def _():
            halo_down(src, dst, stage, mm).start()

    def recv_halo(src, dst, stage, mm):
        @pl.when(has_prev)
        def _():
            halo_down(src, dst, stage, mm).wait_recv()

        @pl.when(has_next)
        def _():
            halo_up(src, dst, stage, mm).wait_recv()

        @pl.when(jnp.logical_not(has_prev))
        def _():
            dst[mm, 0] = jnp.zeros(dst.shape[2:], dst.dtype)

        @pl.when(jnp.logical_not(has_next))
        def _():
            dst[mm, 1] = jnp.zeros(dst.shape[2:], dst.dtype)

    def sent_halo(src, dst, stage, mm):
        @pl.when(has_prev)
        def _():
            halo_up(src, dst, stage, mm).wait_send()

        @pl.when(has_next)
        def _():
            halo_down(src, dst, stage, mm).wait_send()

    last = lp - LANES
    tail = lon - last

    def build(mm, row, value):
        first, end = value[:, :LANES], value[:, last:]
        spot = lax.broadcasted_iota(jnp.int32, end.shape, 1)
        after = pltpu.roll(first, tail, 1)
        before = pltpu.roll(end, LANES - tail, 1)
        wrap = jnp.where(spot < tail, end, jnp.where(spot < tail + half, after, before))
        whole = jnp.concatenate([value[:, :last], wrap], axis=1)
        for s in range(lt):
            d = s - half
            moved = whole if d == 0 else pltpu.roll(whole, (-d) % lp, 1)
            taps_ref[mm, row, pl.ds(s * cp, cp), :] = moved.astype(jnp.bfloat16)

    def flatten(w_ref, flat):
        deep = flat.shape[1]

        def one(t, carry):
            rowblock = jnp.zeros((cp, deep), jnp.float32)
            for s in range(lt):
                block = w_ref[t, s].astype(jnp.float32)
                block = jnp.concatenate(
                    [block, jnp.zeros((cp, deep - block.shape[1]), jnp.float32)], axis=1
                )
                rowblock += pltpu.roll(block, s * cp, 1) if s else block
            flat[pl.ds(pl.multiple_of(t * cp, cp), cp), :] = rowblock.astype(jnp.bfloat16)
            return carry

        lax.fori_loop(0, taps, one, 0)

    def inside(t, i):
        first = offset[sp * rows + i]
        return jnp.where(
            jnp.logical_and(t - reach >= first, t - reach < first + width[sp * rows + i]), 1.0, 0.0
        ).astype(jnp.float32)

    def conv_rows(flat, mm, order):
        for r in order:
            lo, hi = max(0, r - rows + 1), min(taps - 1, r)
            y = jnp.dot(
                flat[lo * cp : (hi + 1) * cp, : lt * cp],
                taps_ref[mm, r],
                preferred_element_type=jnp.float32,
            )
            for t in range(lo, hi + 1):
                i = r - t
                acc[mm, i] += inside(t, i) * y[(t - lo) * cp : (t - lo + 1) * cp]

    def conv_own(own, flat, mm):
        acc[mm] = jnp.zeros(acc.shape[1:], jnp.float32)

        def own_row(r, carry):
            build(mm, reach + r, own[mm, r].astype(jnp.float32))
            return carry

        lax.fori_loop(0, rows, own_row, 0)
        conv_rows(flat, mm, range(reach, reach + rows))

    def conv_rim(halo, flat, mm):
        def rim_row(r, carry):
            build(mm, r, halo[mm, 0, r].astype(jnp.float32))
            build(mm, reach + rows + r, halo[mm, 1, r].astype(jnp.float32))
            return carry

        lax.fori_loop(0, reach, rim_row, 0)
        conv_rows(flat, mm, list(range(reach)) + list(range(reach + rows, 2 * reach + rows)))

    def scaled(mm, i):
        wide = jnp.full((8, LANES), width[sp * rows + i], jnp.int32).astype(jnp.float32)
        return acc[mm, i] * lax.rsqrt(wide)[:1, :1]

    def each(count, body):
        def step(index, carry):
            body(index)
            return carry

        lax.fori_loop(0, count, step, 0)

    def pred_copy(k, j, mm, src_dev, dst_dev):
        return pltpu.make_async_remote_copy(
            src_ref=pred.at[mm, dst_dev * q + j],
            dst_ref=gath.at[src_dev, mm, j],
            send_sem=ps_sem.at[k, j, mm],
            recv_sem=pr_sem.at[k, j, mm],
            device_id={"space": sp, "ens": dst_dev},
            device_id_type=MESH,
        )

    def grad_copy(k, j, mm, src_dev, dst_dev):
        return pltpu.make_async_remote_copy(
            src_ref=grad.at[dst_dev, mm, j],
            dst_ref=o_ref.at[mm, src_dev * q + j],
            send_sem=gs_sem.at[k, j, mm],
            recv_sem=gr_sem.at[k, j, mm],
            device_id={"space": sp, "ens": dst_dev},
            device_id_type=MESH,
        )

    for mm in range(mem):
        send_halo(x_ref, halo1, 0, mm)
    flatten(w1_ref, flat1)
    each(mem, lambda mm: conv_own(x_ref, flat1, mm))
    flatten(w2_ref, flat2)
    for mm in range(mem):
        recv_halo(x_ref, halo1, 0, mm)
        conv_rim(halo1, flat1, mm)

        def hidden_row(i):
            hid[mm, i] = jax.nn.gelu(scaled(mm, i) + b1_ref[...]).astype(jnp.bfloat16)

        each(rows, hidden_row)
        send_halo(hid, halo2, 1, mm)
    each(mem, lambda mm: conv_own(hid, flat2, mm))
    for mm in range(mem):
        recv_halo(hid, halo2, 1, mm)
        conv_rim(halo2, flat2, mm)

        def pred_row(i):
            total = x_ref[mm, i].astype(jnp.float32) + scaled(mm, i) + b2_ref[...]
            pred[mm, i] = total.astype(jnp.bfloat16)

        each(rows, pred_row)
        for j in range(q):
            for k in range(1, n_e):
                pred_copy(k, j, mm, en, peer(k)).start()
        for j in range(q):
            gath[en, mm, j] = pred[mm, en * q + j]
    members = n_e * mem
    for j in range(q):
        for k in range(1, n_e):
            for mm in range(mem):
                pred_copy(k, j, mm, peer(n_e - k), peer(k)).wait_recv()
        scale = weight[0, en * q + j]

        def part(step, carry):
            group, tile = step // (lp // LANES), step % (lp // LANES)
            chan = pl.ds(pl.multiple_of(group * 16, 16), 16)
            lane = pl.ds(pl.multiple_of(tile * LANES, LANES), LANES)
            spots = [(a // mem, a % mem) for a in range(members)]
            vals = [gath[dev, mm, j, chan, lane].astype(jnp.float32) for dev, mm in spots]
            goal = obs_ref[j, chan, lane].astype(jnp.float32)
            sums = [jnp.zeros((16, LANES), jnp.float32) for _ in range(members)]
            for a in range(members):
                for b in range(a + 1, members):
                    d = phi(vals[a] - vals[b])
                    sums[a] = sums[a] + d
                    sums[b] = sums[b] - d
            for a, (dev, mm) in enumerate(spots):
                g = phi(vals[a] - goal) - sums[a] * jnp.float32(1.0 / (members - 1))
                grad[dev, mm, j, chan, lane] = (g * scale).astype(jnp.bfloat16)
            return carry

        lax.fori_loop(0, (cp // 16) * (lp // LANES), part, 0)
        for k in range(1, n_e):
            for mm in range(mem):
                grad_copy(k, j, mm, en, peer(k)).start()
        for mm in range(mem):
            o_ref[mm, en * q + j] = grad[en, mm, j]
    for mm in range(mem):
        sent_halo(x_ref, halo1, 0, mm)
        sent_halo(hid, halo2, 1, mm)
        for j in range(q):
            for k in range(1, n_e):
                pred_copy(k, j, mm, en, peer(k)).wait_send()
                grad_copy(k, j, mm, peer(n_e - k), peer(k)).wait_recv()
                grad_copy(k, j, mm, en, peer(k)).wait_send()


def local(fields, observed, kernel_one, bias_one, kernel_two, bias_two, band_offset, band_width):
    mem, chan, rows, lon = fields.shape
    taps, _, lt, _ = kernel_one.shape
    reach, half = (taps - 1) // 2, (lt - 1) // 2
    n_s, n_e = lax.axis_size("space"), lax.axis_size("ens")
    q = rows // n_e
    cp, lp = ceil_to(chan, 16), ceil_to(lon + 2 * half, LANES)
    sp, en = lax.axis_index("space"), lax.axis_index("ens")
    base = sp * rows

    glob_rows = (base + lax.iota(jnp.int32, rows)).astype(jnp.float32)
    weight = jnp.cos(jnp.pi * (glob_rows + 0.5) / (rows * n_s) - jnp.pi / 2)[None]

    x = jnp.transpose(fields, (0, 2, 1, 3))
    x = jnp.pad(x, ((0, 0), (0, 0), (0, cp - chan), (0, lp - lon)))
    obs = lax.dynamic_slice_in_dim(observed, en * q, q, 1)
    obs = jnp.pad(jnp.transpose(obs, (1, 0, 2)), ((0, 0), (0, cp - chan), (0, lp - lon)))

    def blocks(w):
        w = jnp.transpose(w, (0, 2, 1, 3))
        return jnp.pad(w, ((0, 0), (0, 0), (0, cp - chan), (0, LANES - chan)))

    def column(b):
        return jnp.pad(b, (0, cp - chan))[:, None]

    dims = (n_s, n_e, mem, rows, cp, lon, lp, taps, lt)
    vmem = pl.BlockSpec(memory_space=pltpu.VMEM)
    smem = pl.BlockSpec(memory_space=pltpu.SMEM)
    bf16 = jnp.bfloat16
    deep = ceil_to(lt * cp, LANES)
    out = pl.pallas_call(
        functools.partial(kernel, dims),
        out_shape=jax.ShapeDtypeStruct((mem, rows, cp, lp), bf16),
        in_specs=[smem] * 3 + [vmem] * 6,
        out_specs=vmem,
        scratch_shapes=[
            pltpu.VMEM((taps * cp, deep), bf16),
            pltpu.VMEM((taps * cp, deep), bf16),
            pltpu.VMEM((mem, rows + 2 * reach, lt * cp, lp), bf16),
            pltpu.VMEM((mem, rows, cp, lp), jnp.float32),
            pltpu.VMEM((mem, 2, reach, cp, lp), bf16),
            pltpu.VMEM((mem, rows, cp, lp), bf16),
            pltpu.VMEM((mem, 2, reach, cp, lp), bf16),
            pltpu.VMEM((mem, rows, cp, lp), bf16),
            pltpu.VMEM((n_e, mem, q, cp, lp), bf16),
            pltpu.VMEM((n_e, mem, q, cp, lp), bf16),
            pltpu.SemaphoreType.DMA((2, 2, mem)),
            pltpu.SemaphoreType.DMA((2, 2, mem)),
            pltpu.SemaphoreType.DMA((n_e, q, mem)),
            pltpu.SemaphoreType.DMA((n_e, q, mem)),
            pltpu.SemaphoreType.DMA((n_e, q, mem)),
            pltpu.SemaphoreType.DMA((n_e, q, mem)),
        ],
        compiler_params=pltpu.CompilerParams(
            collective_id=0, has_side_effects=True, vmem_limit_bytes=40 * 1024 * 1024
        ),
    )(
        band_offset,
        band_width,
        weight,
        x,
        obs,
        blocks(kernel_one),
        column(bias_one),
        blocks(kernel_two),
        column(bias_two),
    )
    return jnp.transpose(out[:, :, :chan, :lon], (0, 2, 1, 3))


def solution(mesh):
    in_specs = (P("ens", None, "space", None), P(None, "space", None), P(), P(), P(), P(), P(), P())
    out_specs = P("ens", None, "space", None)
    return jax.shard_map(local, mesh=mesh, in_specs=in_specs, out_specs=out_specs, check_vma=False)
```

```python
import functools

import jax
import jax.numpy as jnp
from jax import lax
from jax.experimental import pallas as pl
from jax.experimental.pallas import tpu as pltpu
from jax.sharding import PartitionSpec as P

MESH = pl.DeviceIdType.MESH
LANES = 128


def ceil_to(value, unit):
    return -(-value // unit) * unit


def phi(diff):
    return diff * lax.rsqrt(diff * diff + jnp.float32(0.25))


def kernel(
    dims,
    offset,
    width,
    weight,
    x_ref,
    obs_ref,
    w1_ref,
    b1_ref,
    w2_ref,
    b2_ref,
    o_ref,
    flat1,
    flat2,
    taps_ref,
    acc,
    halo1,
    hid,
    halo2,
    pred,
    gath,
    grad,
    hs_sem,
    hr_sem,
    ps_sem,
    pr_sem,
    gs_sem,
    gr_sem,
):
    n_s, n_e, mem, rows, cp, lon, lp, taps, lt = dims
    reach = (taps - 1) // 2
    half = (lt - 1) // 2
    q = rows // n_e
    sp = lax.axis_index("space")
    en = lax.axis_index("ens")
    has_prev = sp > 0
    has_next = sp < n_s - 1

    def at_prev():
        return {"space": sp - 1, "ens": en}

    def at_next():
        return {"space": sp + 1, "ens": en}

    def peer(k):
        return lax.rem(en + k, n_e)

    barrier = pltpu.get_barrier_semaphore()

    @pl.when(has_prev)
    def _():
        pl.semaphore_signal(barrier, inc=1, device_id=at_prev(), device_id_type=MESH)

    @pl.when(has_next)
    def _():
        pl.semaphore_signal(barrier, inc=1, device_id=at_next(), device_id_type=MESH)

    for k in range(1, n_e):
        pl.semaphore_signal(
            barrier, inc=1, device_id={"space": sp, "ens": peer(k)}, device_id_type=MESH
        )
    count = n_e - 1 + jnp.where(has_prev, 1, 0) + jnp.where(has_next, 1, 0)
    pl.semaphore_wait(barrier, count)

    def halo_up(src, dst, stage, mm):
        return pltpu.make_async_remote_copy(
            src_ref=src.at[mm, pl.ds(0, reach)],
            dst_ref=dst.at[mm, 1],
            send_sem=hs_sem.at[stage, 0, mm],
            recv_sem=hr_sem.at[stage, 0, mm],
            device_id=at_prev(),
            device_id_type=MESH,
        )

    def halo_down(src, dst, stage, mm):
        return pltpu.make_async_remote_copy(
            src_ref=src.at[mm, pl.ds(rows - reach, reach)],
            dst_ref=dst.at[mm, 0],
            send_sem=hs_sem.at[stage, 1, mm],
            recv_sem=hr_sem.at[stage, 1, mm],
            device_id=at_next(),
            device_id_type=MESH,
        )

    def send_halo(src, dst, stage, mm):
        @pl.when(has_prev)
        def _():
            halo_up(src, dst, stage, mm).start()

        @pl.when(has_next)
        def _():
            halo_down(src, dst, stage, mm).start()

    def recv_halo(src, dst, stage, mm):
        @pl.when(has_prev)
        def _():
            halo_down(src, dst, stage, mm).wait_recv()

        @pl.when(has_next)
        def _():
            halo_up(src, dst, stage, mm).wait_recv()

        @pl.when(jnp.logical_not(has_prev))
        def _():
            dst[mm, 0] = jnp.zeros(dst.shape[2:], dst.dtype)

        @pl.when(jnp.logical_not(has_next))
        def _():
            dst[mm, 1] = jnp.zeros(dst.shape[2:], dst.dtype)

    def sent_halo(src, dst, stage, mm):
        @pl.when(has_prev)
        def _():
            halo_up(src, dst, stage, mm).wait_send()

        @pl.when(has_next)
        def _():
            halo_down(src, dst, stage, mm).wait_send()

    last = lp - LANES
    tail = lon - last

    def build(mm, row, value):
        first, end = value[:, :LANES], value[:, last:]
        spot = lax.broadcasted_iota(jnp.int32, end.shape, 1)
        after = pltpu.roll(first, tail, 1)
        before = pltpu.roll(end, LANES - tail, 1)
        wrap = jnp.where(spot < tail, end, jnp.where(spot < tail + half, after, before))
        whole = jnp.concatenate([value[:, :last], wrap], axis=1)
        for s in range(lt):
            d = s - half
            moved = whole if d == 0 else pltpu.roll(whole, (-d) % lp, 1)
            taps_ref[mm, row, pl.ds(s * cp, cp), :] = moved.astype(jnp.bfloat16)

    def flatten(w_ref, flat):
        deep = flat.shape[1]

        def one(t, carry):
            rowblock = jnp.zeros((cp, deep), jnp.float32)
            for s in range(lt):
                block = w_ref[t, s].astype(jnp.float32)
                block = jnp.concatenate(
                    [block, jnp.zeros((cp, deep - block.shape[1]), jnp.float32)], axis=1
                )
                rowblock += pltpu.roll(block, s * cp, 1) if s else block
            flat[pl.ds(pl.multiple_of(t * cp, cp), cp), :] = rowblock.astype(jnp.bfloat16)
            return carry

        lax.fori_loop(0, taps, one, 0)

    def inside(t, i):
        first = offset[sp * rows + i]
        return jnp.where(
            jnp.logical_and(t - reach >= first, t - reach < first + width[sp * rows + i]), 1.0, 0.0
        ).astype(jnp.float32)

    def conv_rows(flat, mm, order):
        for r in order:
            lo, hi = max(0, r - rows + 1), min(taps - 1, r)
            y = jnp.dot(
                flat[lo * cp : (hi + 1) * cp, : lt * cp],
                taps_ref[mm, r],
                preferred_element_type=jnp.float32,
            )
            for t in range(lo, hi + 1):
                i = r - t
                acc[mm, i] += inside(t, i) * y[(t - lo) * cp : (t - lo + 1) * cp]

    def conv_own(own, flat, mm):
        acc[mm] = jnp.zeros(acc.shape[1:], jnp.float32)

        def own_row(r, carry):
            build(mm, reach + r, own[mm, r].astype(jnp.float32))
            return carry

        lax.fori_loop(0, rows, own_row, 0)
        conv_rows(flat, mm, range(reach, reach + rows))

    def conv_rim(halo, flat, mm):
        def rim_row(r, carry):
            build(mm, r, halo[mm, 0, r].astype(jnp.float32))
            build(mm, reach + rows + r, halo[mm, 1, r].astype(jnp.float32))
            return carry

        lax.fori_loop(0, reach, rim_row, 0)
        conv_rows(flat, mm, list(range(reach)) + list(range(reach + rows, 2 * reach + rows)))

    def scaled(mm, i):
        wide = jnp.full((8, LANES), width[sp * rows + i], jnp.int32).astype(jnp.float32)
        return acc[mm, i] * lax.rsqrt(wide)[:1, :1]

    def each(count, body):
        def step(index, carry):
            body(index)
            return carry

        lax.fori_loop(0, count, step, 0)

    def pred_copy(k, j, mm, src_dev, dst_dev):
        return pltpu.make_async_remote_copy(
            src_ref=pred.at[mm, dst_dev * q + j],
            dst_ref=gath.at[src_dev, mm, j],
            send_sem=ps_sem.at[k, j, mm],
            recv_sem=pr_sem.at[k, j, mm],
            device_id={"space": sp, "ens": dst_dev},
            device_id_type=MESH,
        )

    def grad_copy(k, j, mm, src_dev, dst_dev):
        return pltpu.make_async_remote_copy(
            src_ref=grad.at[dst_dev, mm, j],
            dst_ref=o_ref.at[mm, src_dev * q + j],
            send_sem=gs_sem.at[k, j, mm],
            recv_sem=gr_sem.at[k, j, mm],
            device_id={"space": sp, "ens": dst_dev},
            device_id_type=MESH,
        )

    for mm in range(mem):
        send_halo(x_ref, halo1, 0, mm)
    flatten(w1_ref, flat1)
    for mm in range(mem):
        conv_own(x_ref, flat1, mm)
        recv_halo(x_ref, halo1, 0, mm)
        conv_rim(halo1, flat1, mm)

        def hidden_row(i):
            hid[mm, i] = jax.nn.gelu(scaled(mm, i) + b1_ref[...]).astype(jnp.bfloat16)

        each(rows, hidden_row)
        send_halo(hid, halo2, 1, mm)
    flatten(w2_ref, flat2)
    for mm in range(mem):
        conv_own(hid, flat2, mm)
        recv_halo(hid, halo2, 1, mm)
        conv_rim(halo2, flat2, mm)

        def pred_row(i):
            total = x_ref[mm, i].astype(jnp.float32) + scaled(mm, i) + b2_ref[...]
            pred[mm, i] = total.astype(jnp.bfloat16)

        each(rows, pred_row)
        for j in range(q):
            for k in range(1, n_e):
                pred_copy(k, j, mm, en, peer(k)).start()
        for j in range(q):
            gath[en, mm, j] = pred[mm, en * q + j]
    members = n_e * mem
    for j in range(q):
        for k in range(1, n_e):
            for mm in range(mem):
                pred_copy(k, j, mm, peer(n_e - k), peer(k)).wait_recv()
        scale = weight[0, en * q + j]

        def part(step, carry):
            group, tile = step // (lp // LANES), step % (lp // LANES)
            chan = pl.ds(pl.multiple_of(group * 16, 16), 16)
            lane = pl.ds(pl.multiple_of(tile * LANES, LANES), LANES)
            spots = [(a // mem, a % mem) for a in range(members)]
            vals = [gath[dev, mm, j, chan, lane].astype(jnp.float32) for dev, mm in spots]
            goal = obs_ref[j, chan, lane].astype(jnp.float32)
            sums = [jnp.zeros((16, LANES), jnp.float32) for _ in range(members)]
            for a in range(members):
                for b in range(a + 1, members):
                    d = phi(vals[a] - vals[b])
                    sums[a] = sums[a] + d
                    sums[b] = sums[b] - d
            for a, (dev, mm) in enumerate(spots):
                g = phi(vals[a] - goal) - sums[a] * jnp.float32(1.0 / (members - 1))
                grad[dev, mm, j, chan, lane] = (g * scale).astype(jnp.bfloat16)
            return carry

        lax.fori_loop(0, (cp // 16) * (lp // LANES), part, 0)
        for k in range(1, n_e):
            for mm in range(mem):
                grad_copy(k, j, mm, en, peer(k)).start()
        for mm in range(mem):
            o_ref[mm, en * q + j] = grad[en, mm, j]
    for mm in range(mem):
        sent_halo(x_ref, halo1, 0, mm)
        sent_halo(hid, halo2, 1, mm)
        for j in range(q):
            for k in range(1, n_e):
                pred_copy(k, j, mm, en, peer(k)).wait_send()
                grad_copy(k, j, mm, peer(n_e - k), peer(k)).wait_recv()
                grad_copy(k, j, mm, en, peer(k)).wait_send()


def local(fields, observed, kernel_one, bias_one, kernel_two, bias_two, band_offset, band_width):
    mem, chan, rows, lon = fields.shape
    taps, _, lt, _ = kernel_one.shape
    reach, half = (taps - 1) // 2, (lt - 1) // 2
    n_s, n_e = lax.axis_size("space"), lax.axis_size("ens")
    q = rows // n_e
    cp, lp = ceil_to(chan, 16), ceil_to(lon + 2 * half, LANES)
    sp, en = lax.axis_index("space"), lax.axis_index("ens")
    base = sp * rows

    glob_rows = (base + lax.iota(jnp.int32, rows)).astype(jnp.float32)
    weight = jnp.cos(jnp.pi * (glob_rows + 0.5) / (rows * n_s) - jnp.pi / 2)[None]

    x = jnp.transpose(fields, (0, 2, 1, 3))
    x = jnp.pad(x, ((0, 0), (0, 0), (0, cp - chan), (0, lp - lon)))
    obs = lax.dynamic_slice_in_dim(observed, en * q, q, 1)
    obs = jnp.pad(jnp.transpose(obs, (1, 0, 2)), ((0, 0), (0, cp - chan), (0, lp - lon)))

    def blocks(w):
        w = jnp.transpose(w, (0, 2, 1, 3))
        return jnp.pad(w, ((0, 0), (0, 0), (0, cp - chan), (0, LANES - chan)))

    def column(b):
        return jnp.pad(b, (0, cp - chan))[:, None]

    dims = (n_s, n_e, mem, rows, cp, lon, lp, taps, lt)
    vmem = pl.BlockSpec(memory_space=pltpu.VMEM)
    smem = pl.BlockSpec(memory_space=pltpu.SMEM)
    bf16 = jnp.bfloat16
    deep = ceil_to(lt * cp, LANES)
    out = pl.pallas_call(
        functools.partial(kernel, dims),
        out_shape=jax.ShapeDtypeStruct((mem, rows, cp, lp), bf16),
        in_specs=[smem] * 3 + [vmem] * 6,
        out_specs=vmem,
        scratch_shapes=[
            pltpu.VMEM((taps * cp, deep), bf16),
            pltpu.VMEM((taps * cp, deep), bf16),
            pltpu.VMEM((mem, rows + 2 * reach, lt * cp, lp), bf16),
            pltpu.VMEM((mem, rows, cp, lp), jnp.float32),
            pltpu.VMEM((mem, 2, reach, cp, lp), bf16),
            pltpu.VMEM((mem, rows, cp, lp), bf16),
            pltpu.VMEM((mem, 2, reach, cp, lp), bf16),
            pltpu.VMEM((mem, rows, cp, lp), bf16),
            pltpu.VMEM((n_e, mem, q, cp, lp), bf16),
            pltpu.VMEM((n_e, mem, q, cp, lp), bf16),
            pltpu.SemaphoreType.DMA((2, 2, mem)),
            pltpu.SemaphoreType.DMA((2, 2, mem)),
            pltpu.SemaphoreType.DMA((n_e, q, mem)),
            pltpu.SemaphoreType.DMA((n_e, q, mem)),
            pltpu.SemaphoreType.DMA((n_e, q, mem)),
            pltpu.SemaphoreType.DMA((n_e, q, mem)),
        ],
        compiler_params=pltpu.CompilerParams(
            collective_id=0, has_side_effects=True, vmem_limit_bytes=40 * 1024 * 1024
        ),
    )(
        band_offset,
        band_width,
        weight,
        x,
        obs,
        blocks(kernel_one),
        column(bias_one),
        blocks(kernel_two),
        column(bias_two),
    )
    return jnp.transpose(out[:, :, :chan, :lon], (0, 2, 1, 3))


def solution(mesh):
    in_specs = (P("ens", None, "space", None), P(None, "space", None), P(), P(), P(), P(), P(), P())
    out_specs = P("ens", None, "space", None)
    return jax.shard_map(local, mesh=mesh, in_specs=in_specs, out_specs=out_specs, check_vma=False)
```
